32 devices in a mesh: row: 4 (over x, core), col: 8 (over z, y).
Axes of the slice: x: 2, y: 2, z: 4, core: 2. Of those that a mesh axis runs over, the one named last changes fastest.
Arguments:
- local_load: float32 [4, 8, 1024, 256], P('row', 'col'), may hold values from -6 to 6
- schur_operator: float32 [4, 8, 1024, 1024], P('row', 'col'), may hold values from -1 to 5
- local_solver: float32 [4, 8, 1024, 1024], P('row', 'col'), may hold values from -1 to 1
- coarse_modes: float32 [4, 8, 32, 1024], P('row', 'col'), may hold values from -0.1875 to 0.1875
- coarse_inverse: float32 [4, 8, 4, 32, 256], P('row', 'col'), may hold values from -1 to 2
- share_rows: int32 [4, 8, 3, 3, 128], P('row', 'col'), may hold values from 0 to 1023, as said below
- share_count: int32 [4, 8, 3, 3], P('row', 'col'), may hold values from 0 to 128, as said below
- multiplicity: int32 [4, 8, 1024], P('row', 'col'), may hold values from 1 to 2, as said below
Outputs:
- iterate: float32 [4, 8, 1024, 256], P('row', 'col')
- residual: float32 [4, 8, 1024, 256], P('row', 'col')
The draws below stay inside these ranges and needn't reach their ends.
Inputs may be any that keep to these rules, and one draw needn't show every extreme that they name: `share_rows`: within one subdomain no row lies in two lists, and only the first share_count entries of a list are meaningful. Entry m of the list of (a, b) toward (a + p - 1, b + q - 1) and entry m of that neighbour's list toward (a, b) name the same interface unknown. share_count[a, b, p, q] equals the neighbour's count toward (a, b); it is 0 for the centre and where no neighbour exists, at most 128 along a grid axis and at most 16 for a diagonal neighbour, and both bounds are reached. multiplicity is 2 on rows that lie in some list and 1 elsewhere.
All inputs are finite; a program needn't handle non-finite values.
Results may differ from the reference program's by a relative error of at most 0.0003.
Values sent between devices are 32-bit elements; how exact they have to be, the bound alone decides.
A program may use at most 128 MiB of HBM per device.

```python
import math
import jax
import jax.numpy as jnp
import numpy as np
from jax import lax

NI = 1024
R = 256
MODES = 32
SHARE = 128
CORNER = 16
STEPS = 2
GRID_ROWS = 4
GRID_COLS = 8


def shifted_drawn(array_in, row_by, col_by):
    row_count, col_count = (array_in.shape[0], array_in.shape[1])
    padded = jnp.pad(array_in, ((1, 1), (1, 1)) + ((0, 0),) * (array_in.ndim - 2))
    return padded[1 - row_by:1 - row_by + row_count, 1 - col_by:1 - col_by + col_count]


def slot_layout():
    starts = np.array([[4 * SHARE, 0, 4 * SHARE + CORNER], [SHARE, 0, 2 * SHARE], [4 * SHARE + 2 * CORNER, 3 * SHARE, 4 * SHARE + 3 * CORNER]], np.int32)
    slot_sizes = np.array([[CORNER, SHARE, CORNER], [SHARE, 0, SHARE], [CORNER, SHARE, CORNER]], np.int32)
    return (starts, slot_sizes)


def sharing(key):
    base_key = jax.random.fold_in(key, 7)
    perm_key, face_key, corner_key, filler_key = jax.random.split(base_key, 4)
    perm_keys = jax.random.split(perm_key, GRID_ROWS * GRID_COLS)
    permutations = jax.vmap(lambda sub_key: jax.random.permutation(sub_key, NI))(perm_keys)
    permutations = permutations.reshape(GRID_ROWS, GRID_COLS, NI).astype(jnp.int32)
    face_counts = jax.random.randint(face_key, (GRID_ROWS, GRID_COLS, 2), SHARE // 2, SHARE + 1).astype(jnp.int32)
    corner_counts = jax.random.randint(corner_key, (GRID_ROWS, GRID_COLS, 2), 1, CORNER + 1).astype(jnp.int32)
    face_counts = face_counts.at[0, 0, 0].set(SHARE)
    corner_counts = corner_counts.at[0, 0, 0].set(CORNER)
    row_ids = jnp.arange(GRID_ROWS)[:, None]
    col_ids = jnp.arange(GRID_COLS)[None, :]
    east_counts = jnp.where(col_ids < GRID_COLS - 1, face_counts[:, :, 0], 0)
    south_counts = jnp.where(row_ids < GRID_ROWS - 1, face_counts[:, :, 1], 0)
    south_east = jnp.where((row_ids < GRID_ROWS - 1) & (col_ids < GRID_COLS - 1), corner_counts[:, :, 0], 0)
    south_west = jnp.where((row_ids < GRID_ROWS - 1) & (col_ids > 0), corner_counts[:, :, 1], 0)
    no_counts = jnp.zeros_like(east_counts)
    count_table = [[shifted_drawn(south_east, 1, 1), shifted_drawn(south_counts, 1, 0), shifted_drawn(south_west, 1, -1)], [shifted_drawn(east_counts, 0, 1), no_counts, east_counts], [south_west, south_counts, south_east]]
    counts = jnp.stack([jnp.stack(count_line, axis=-1) for count_line in count_table], axis=-2).astype(jnp.int32)
    starts, slot_sizes = slot_layout()
    slot_ids = np.arange(SHARE, dtype=np.int32)
    positions = starts[:, :, None] + np.minimum(slot_ids[None, None, :], np.maximum(slot_sizes - 1, 0)[:, :, None])
    listed = permutations[:, :, positions]
    filler = jax.random.randint(filler_key, listed.shape, 0, NI).astype(jnp.int32)
    share_rows = jnp.where(jnp.asarray(slot_ids) < counts[..., None], listed, filler).astype(jnp.int32)
    slot_iota = jnp.arange(NI, dtype=jnp.int32)
    shared_flag = jnp.zeros((GRID_ROWS, GRID_COLS, NI), jnp.int32)
    for row_slot in range(3):
        for col_slot in range(3):
            first_slot = int(starts[row_slot, col_slot])
            used_count = counts[:, :, row_slot, col_slot][:, :, None]
            inside = (slot_iota >= first_slot) & (slot_iota < first_slot + used_count)
            shared_flag = shared_flag + inside.astype(jnp.int32)
    inverse_perm = jnp.argsort(permutations, axis=-1).astype(jnp.int32)
    multiplicity = jnp.take_along_axis(1 + shared_flag, inverse_perm, axis=-1).astype(jnp.int32)
    return (share_rows, counts, multiplicity)


def draw_share_rows(key, part):
    return sharing(key)[0]


def draw_share_count(key, part):
    return sharing(key)[1]


def draw_multiplicity(key, part):
    return sharing(key)[2]


def operator_noise(noise_key):
    full_shape = (GRID_ROWS, GRID_COLS, NI, NI)
    return jnp.clip(jax.random.normal(noise_key, full_shape, jnp.float32), -5.0, 5.0)


def diagonal_values(key):
    base_key = jax.random.fold_in(key, 19)
    return jax.random.uniform(base_key, (GRID_ROWS, GRID_COLS, NI), jnp.float32, 2.0, 4.0)


def draw_schur_operator(key, part):
    diagonal = diagonal_values(key)
    noise_key = jax.random.fold_in(jax.random.fold_in(key, 29), 0)
    identity = jnp.eye(NI, dtype=jnp.float32)
    return identity * diagonal[..., None] + 0.5 / math.sqrt(NI) * operator_noise(noise_key)


def draw_local_solver(key, part):
    diagonal = diagonal_values(key)
    noise_key = jax.random.fold_in(jax.random.fold_in(key, 31), 0)
    identity = jnp.eye(NI, dtype=jnp.float32)
    return identity * (1.0 / diagonal)[..., None] + 0.1 / math.sqrt(NI) * operator_noise(noise_key)


def draw_coarse_inverse(key, part):
    base_key = jax.random.fold_in(key, 23)
    noise_key, diag_key = jax.random.split(base_key)
    tile_width = GRID_COLS * MODES
    full_shape = (GRID_ROWS, GRID_COLS, GRID_ROWS, MODES, tile_width)
    noise_scale = 0.5 / math.sqrt(MODES * GRID_ROWS * GRID_COLS)
    noise_one = jnp.clip(jax.random.normal(noise_key, full_shape, jnp.float32), -5.0, 5.0)
    same_row = lax_iota(full_shape, 0) == lax_iota(full_shape, 2)
    same_col = lax_iota(full_shape, 4) == lax_iota(full_shape, 1) * MODES + lax_iota(full_shape, 3)
    diagonal = jax.random.uniform(diag_key, full_shape, jnp.float32, 0.5, 1.0)
    return noise_one * noise_scale + jnp.where(same_row & same_col, diagonal, 0.0)


def lax_iota(full_shape, dimension):
    return jax.lax.broadcasted_iota(jnp.int32, full_shape, dimension)


def level_of(stream_key, extent, shards, smallest, high):
    def one(dim, parts):
        steps = jax.random.uniform(jax.random.fold_in(jax.random.fold_in(stream_key, 6), dim), (parts,), jnp.float32, smallest / len(shards), high / len(shards))
        return jnp.repeat(jnp.exp(steps), extent[dim] // parts).reshape((-1,) + (1,) * (len(extent) - dim - 1))

    level = one(*shards[0])
    for cut in shards[1:]:
        level = level * one(*cut)
    return level


def gaussian(stream_key, shape, scale, reach, shards=(), held_as=jnp.bfloat16):
    result = jax.random.normal(stream_key, shape, jnp.float32) * scale
    if len(shards) > 0:
        result = level_of(stream_key, shape, shards, -0.22, 0.18) * result
    return jnp.clip(result, min=-reach, max=reach).astype(held_as)


def setup_inputs(seed: int = 0) -> dict:
    key_of = jax.random.split(jax.random.key(seed), 9)
    return {
        "local_load": gaussian(key_of[0], (GRID_ROWS, GRID_COLS, NI, R), 1.0, 6.0, ((0, 4), (1, 8)), jnp.float32),
        "schur_operator": draw_schur_operator(jax.random.fold_in(key_of[8], 71), 0),
        "local_solver": draw_local_solver(jax.random.fold_in(key_of[8], 71), 0),
        "coarse_modes": gaussian(key_of[3], (GRID_ROWS, GRID_COLS, MODES, NI), NI ** -0.5, 0.1875, ((0, 4), (1, 8)), jnp.float32),
        "coarse_inverse": draw_coarse_inverse(jax.random.fold_in(key_of[8], 71), 0),
        "share_rows": draw_share_rows(jax.random.fold_in(key_of[8], 71), 0),
        "share_count": draw_share_count(jax.random.fold_in(key_of[8], 71), 0),
        "multiplicity": draw_multiplicity(jax.random.fold_in(key_of[8], 71), 0),
    }


PRECISE = lax.Precision.HIGHEST


def shifted(array_in, row_by, col_by):
    row_count, col_count = array_in.shape[0], array_in.shape[1]
    padded = jnp.pad(array_in, ((1, 1), (1, 1)) + ((0, 0),) * (array_in.ndim - 2))
    return padded[1 - row_by:1 - row_by + row_count, 1 - col_by:1 - col_by + col_count]


def pick_rows(values, indices):
    return values[indices]


def add_rows(values, indices, arrived):
    return values.at[indices.reshape(-1)].add(arrived.reshape(-1, arrived.shape[-1]))


def assemble(values, share_rows, share_count):
    slot_ids = jnp.arange(share_rows.shape[-1], dtype=jnp.int32)
    live_mask = (slot_ids < share_count[..., None]).astype(values.dtype)
    packets = jax.vmap(jax.vmap(pick_rows))(values, share_rows) * live_mask[..., None]
    count_lines = []
    for row_slot in range(3):
        count_line = []
        for col_slot in range(3):
            count_line.append(shifted(packets[:, :, 2 - row_slot, 2 - col_slot], 1 - row_slot, 1 - col_slot))
        count_lines.append(jnp.stack(count_line, axis=2))
    incoming = jnp.stack(count_lines, axis=2)
    return jax.vmap(jax.vmap(add_rows))(values, share_rows, incoming)


def apply_matrix(matrix, vector):
    return jnp.einsum('abij,abjr->abir', matrix, vector, precision=PRECISE)


def reference(local_load, schur_operator, local_solver, coarse_modes, coarse_inverse, share_rows, share_count, multiplicity):
    weight = (1.0 / multiplicity.astype(jnp.float32))[..., None]
    residual = assemble(local_load, share_rows, share_count)
    iterate = jnp.zeros_like(residual)
    for step_index in range(STEPS):
        coarse_rhs = jnp.einsum('abmi,abir->abmr', coarse_modes, weight * residual, precision=PRECISE)
        coarse_sol = jnp.einsum('abcmk,cbmr->akr', coarse_inverse, coarse_rhs, precision=PRECISE)
        coarse_sol = coarse_sol.reshape(GRID_ROWS, GRID_COLS, MODES, coarse_sol.shape[-1])
        spread_values = weight * jnp.einsum('abmi,abmr->abir', coarse_modes, coarse_sol, precision=PRECISE)
        correction = assemble(spread_values, share_rows, share_count)
        iterate = iterate + correction
        residual = residual - assemble(apply_matrix(schur_operator, correction), share_rows, share_count)
        update = assemble(weight * apply_matrix(local_solver, weight * residual), share_rows, share_count)
        iterate = iterate + update
        residual = residual - assemble(apply_matrix(schur_operator, update), share_rows, share_count)
    return iterate, residual
```

```python
import functools

import jax
import jax.numpy as jnp
from jax import lax
from jax.experimental import pallas as pl
from jax.experimental.pallas import tpu as pltpu
from jax.sharding import PartitionSpec as P

CORNER = 16
STEPS = 2
F32 = jnp.float32
BF16 = jnp.bfloat16
MESH = pl.DeviceIdType.MESH

DIRS = ((-1, 0), (0, -1), (0, 1), (1, 0), (-1, -1), (-1, 1), (1, -1), (1, 1))
OPPOSITE = (3, 2, 1, 0, 7, 6, 5, 4)
LANES = 128


def split(value):
    high = value.astype(BF16)
    low = (value - high.astype(F32)).astype(BF16)
    return high, low


def dot(left, right):
    return jnp.dot(left, right, preferred_element_type=F32)


def dot3(left, right):
    (lh, ll), (rh, rl) = left, right
    return dot(lh, rh) + (dot(lh, rl) + dot(ll, rh))


def pick(onehot, value):
    high, low = value
    return dot(onehot, high) + dot(onehot, low)


def kernel(
    rows, cols, n, r, k, share,
    load_ref, schur_hbm, solver_hbm, modes_ref, tile_ref, slots_ref, weight_ref,
    iter_ref, res_ref,
    mat_s, mat_m, s_hi, s_lo, m_hi, m_lo, gather_ref, scatter_ref,
    wide_ref, ext_hi, ext_lo, ext_t_hi, ext_t_lo, cor_hi, cor_lo, cor_t_hi, cor_t_lo,
    tile_t_hi, tile_t_lo, local_ref,
    mode_send, mode_recv, a_send, a_recv, x_send, x_recv, gat, part, red,
    local_sem, mode_ss, mode_rs, a_ss, a_rs, x_ss, x_rs, g_ss, g_rs, p_ss, p_rs,
):
    a = lax.axis_index("row")
    b = lax.axis_index("col")
    copy_s = pltpu.make_async_copy(schur_hbm, mat_s, local_sem.at[0])
    copy_m = pltpu.make_async_copy(solver_hbm, mat_m, local_sem.at[1])
    copy_s.start()
    copy_m.start()

    def exists(d):
        p, q = a + DIRS[d][0], b + DIRS[d][1]
        return (p >= 0) & (p < rows) & (q >= 0) & (q < cols)

    def there(d):
        return (a + DIRS[d][0], b + DIRS[d][1])

    mode_recv[...] = jnp.zeros_like(mode_recv)
    a_recv[...] = jnp.zeros_like(a_recv)
    x_recv[...] = jnp.zeros_like(x_recv)

    barrier = pltpu.get_barrier_semaphore()
    for off in range(1, rows):
        pl.semaphore_signal(
            barrier, inc=1, device_id=(lax.rem(a + off, rows), b), device_id_type=MESH
        )
    for off in range(1, cols):
        pl.semaphore_signal(
            barrier, inc=1, device_id=(a, lax.rem(b + off, cols)), device_id_type=MESH
        )
    for d in range(4, 8):
        @pl.when(exists(d))
        def _():
            pl.semaphore_signal(barrier, inc=1, device_id=there(d), device_id_type=MESH)

    slot_pad = slots_ref.shape[1]
    slots = slots_ref[...]
    scatter_ref[...] = jnp.where(
        lax.broadcasted_iota(jnp.int32, (n, slot_pad), 0).astype(F32) == slots, 1.0, 0.0
    ).astype(BF16)
    slots_t = jnp.broadcast_to(slots, (LANES, slot_pad)).T
    for i in range(n // LANES):
        ids = (lax.broadcasted_iota(jnp.int32, (slot_pad, LANES), 1) + i * LANES).astype(F32)
        gather_ref[:, i * LANES:(i + 1) * LANES] = jnp.where(ids == slots_t, 1.0, 0.0).astype(BF16)
    weight = weight_ref[...]
    weight_t = jnp.broadcast_to(weight, (LANES, n)).T
    for i in range(r // LANES):
        wide_ref[:, i * LANES:(i + 1) * LANES] = weight_t
    zw = modes_ref[...] * weight
    zw2 = split(zw)
    at_slots = pick_right(zw2, scatter_ref)
    for d in range(4):
        mode_send[d] = at_slots[:, d * share:(d + 1) * share]

    diagonals = sum(exists(d).astype(jnp.int32) for d in range(4, 8))
    pl.semaphore_wait(barrier, rows + cols - 2 + diagonals)

    def mode_copy(d, out):
        e = OPPOSITE[d]
        return pltpu.make_async_remote_copy(
            src_ref=mode_send.at[d],
            dst_ref=mode_recv.at[e if out else d],
            send_sem=mode_ss.at[d],
            recv_sem=mode_rs.at[e if out else d],
            device_id=there(d),
            device_id_type=MESH,
        )

    def for_dirs(count, body):
        for d in range(count):
            @pl.when(exists(d))
            def _():
                body(d)

    for_dirs(4, lambda d: mode_copy(d, True).start())

    def exchange(send, recv, ss, rs, wide):
        def span(d):
            if d < 4:
                return pl.ds(d * wide, wide)
            return pl.ds(4 * wide + (d - 4) * CORNER, CORNER)

        def copy(d, out):
            e = OPPOSITE[d] if out else d
            return pltpu.make_async_remote_copy(
                src_ref=send.at[span(d)],
                dst_ref=recv.at[span(e)],
                send_sem=ss.at[d],
                recv_sem=rs.at[e],
                device_id=there(d),
                device_id_type=MESH,
            )

        def start():
            for_dirs(8, lambda d: copy(d, True).start())

        def wait():
            for_dirs(8, lambda d: copy(d, False).wait_recv())
            for_dirs(8, lambda d: copy(d, True).wait_send())

        return start, wait

    slot_count = 4 * share + 4 * CORNER
    corner_g = gather_ref[4 * share:slot_count, :]
    corner_m = pick(corner_g, split(zw.T))
    c_hi, c_lo = split(corner_m)
    cor_hi[...] = c_hi
    cor_lo[...] = c_lo
    t_hi, t_lo = split(corner_m.T)
    cor_t_hi[...] = t_hi
    cor_t_lo[...] = t_lo
    t_hi, t_lo = split(tile_ref[...].T)
    tile_t_hi[...] = t_hi
    tile_t_lo[...] = t_lo
    local_ref[...] = -load_ref[...]
    iter_ref[...] = jnp.zeros_like(iter_ref)
    res_ref[...] = jnp.zeros_like(res_ref)

    copy_s.wait()
    hi, lo = split(mat_s[...])
    s_hi[...] = hi
    s_lo[...] = lo
    for_dirs(4, lambda d: mode_copy(d, False).wait_recv())
    for_dirs(4, lambda d: mode_copy(d, True).wait_send())

    ext_hi[0:k, :] = zw2[0]
    ext_lo[0:k, :] = zw2[1]
    for d in range(4):
        m_h, m_l = split(mode_recv[d])
        onehot = gather_ref[d * share:(d + 1) * share, :]
        ext_hi[(d + 1) * k:(d + 2) * k, :] = dot(m_h, onehot).astype(BF16)
        ext_lo[(d + 1) * k:(d + 2) * k, :] = dot(m_l, onehot).astype(BF16)
    ext_hi[5 * k:, :] = corner_g
    ext_lo[5 * k:, :] = jnp.zeros_like(corner_g)
    ext_t_hi[...] = ext_hi[...].astype(F32).T.astype(BF16)
    ext_t_lo[...] = ext_lo[...].astype(F32).T.astype(BF16)

    copy_m.wait()
    hi, lo = split(mat_m[...])
    m_hi[...] = hi
    m_lo[...] = lo

    def assemble(value, index):
        send, recv = a_send.at[index], a_recv.at[index]
        start, wait = exchange(send, recv, a_ss.at[index], a_rs.at[index], share)
        send[...] = pick(gather_ref[0:slot_count, :], split(value))
        start()

        def finish():
            wait()
            return value + pick(scatter_ref[...], split(recv[...]))

        return finish

    def step(t, carry):
        gat_t, part_t, red_t = gat.at[t], part.at[t], red.at[t]
        first = split(local_ref[...])
        out = dot3((ext_hi[...], ext_lo[...]), first)
        send, recv = x_send.at[2 * t], x_recv.at[2 * t]
        start, wait = exchange(send, recv, x_ss.at[2 * t], x_rs.at[2 * t], k)
        send[...] = out[k:, :]
        start()
        own = dot3((ext_hi[0:k, :], ext_lo[0:k, :]), split(res_ref[...])) - out[0:k, :]
        wait()
        near = recv[0:k, :]
        for d in range(1, 4):
            near = near + recv[d * k:(d + 1) * k, :]
        near = near + dot3((cor_t_hi[...], cor_t_lo[...]), split(recv[4 * k:, :]))
        gat_t[a] = own - near

        def gather_copy(off, out):
            peer = lax.rem(a + off, rows) if out else lax.rem(a + rows - off, rows)
            return pltpu.make_async_remote_copy(
                src_ref=gat_t.at[a],
                dst_ref=gat_t.at[a if out else peer],
                send_sem=g_ss.at[t, off],
                recv_sem=g_rs.at[t, off],
                device_id=(peer, b),
                device_id_type=MESH,
            )

        for off in range(1, rows):
            gather_copy(off, True).start()
        for off in range(1, rows):
            gather_copy(off, False).wait_recv()
        for off in range(1, rows):
            gather_copy(off, True).wait_send()
        rhs = split(gat_t[...].reshape(rows * k, r))
        part_t[...] = dot3((tile_t_hi[...], tile_t_lo[...]), rhs).reshape(cols, k, r)

        def part_copy(off, out):
            peer = lax.rem(b + off, cols) if out else lax.rem(b + cols - off, cols)
            return pltpu.make_async_remote_copy(
                src_ref=part_t.at[peer],
                dst_ref=red_t.at[off],
                send_sem=p_ss.at[t, off],
                recv_sem=p_rs.at[t, off],
                device_id=(a, peer),
                device_id_type=MESH,
            )

        for off in range(1, cols):
            part_copy(off, True).start()
        sol = part_t[b]
        for off in range(1, cols):
            part_copy(off, False).wait_recv()
            sol = sol + red_t[off]
        for off in range(1, cols):
            part_copy(off, True).wait_send()

        send, recv = x_send.at[2 * t + 1], x_recv.at[2 * t + 1]
        start, wait = exchange(send, recv, x_ss.at[2 * t + 1], x_rs.at[2 * t + 1], k)
        for d in range(4):
            send[d * k:(d + 1) * k, :] = sol
        sol2 = split(sol)
        send[4 * k:, :] = dot3((cor_hi[...], cor_lo[...]), sol2)
        start()
        wait()
        all_sol = split(jnp.concatenate([sol, recv[...]], axis=0))
        corr = dot3((ext_t_hi[...], ext_t_lo[...]), all_sol)
        iter_ref[...] += corr
        moved = local_ref[...] + dot3((s_hi[...], s_lo[...]), split(corr))
        res_ref[...] -= assemble(moved, 2 * t)()
        weighted = split(wide_ref[...] * res_ref[...])
        update = assemble(
            wide_ref[...] * dot3((m_hi[...], m_lo[...]), weighted), 2 * t + 1
        )()
        iter_ref[...] += update
        local_ref[...] = dot3((s_hi[...], s_lo[...]), split(update))
        return carry

    lax.fori_loop(0, STEPS, step, 0)
    res_ref[...] -= assemble(local_ref[...], 2 * STEPS)()


def pick_right(value, onehot_ref):
    return dot(value[0], onehot_ref[...]) + dot(value[1], onehot_ref[...])


def on_device(
    rows, cols,
    local_load,
    schur_operator,
    local_solver,
    coarse_modes,
    coarse_inverse,
    share_rows,
    share_count,
    multiplicity,
):
    n, r = local_load.shape[2:]
    k = coarse_modes.shape[2]
    share = share_rows.shape[-1]
    live = lax.broadcasted_iota(jnp.int32, share_rows.shape[2:], 2) < share_count[0, 0][..., None]
    listed = jnp.where(live, share_rows[0, 0], -1).astype(F32)
    pieces = [
        listed[p + 1, q + 1, : share if d < 4 else CORNER] for d, (p, q) in enumerate(DIRS)
    ]
    slot_count = 4 * share + 4 * CORNER
    slot_pad = -(-slot_count // LANES) * LANES
    slots = jnp.pad(jnp.concatenate(pieces), (0, slot_pad - slot_count), constant_values=-1.0)
    weight = 1.0 / multiplicity[0, 0].astype(F32)
    width = 5 * k + 4 * CORNER
    vm = pltpu.VMEM
    dma = pltpu.SemaphoreType.DMA
    scratch = [
        vm((n, n), F32), vm((n, n), F32),
        vm((n, n), BF16), vm((n, n), BF16), vm((n, n), BF16), vm((n, n), BF16),
        vm((slot_pad, n), BF16), vm((n, slot_pad), BF16),
        vm((n, r), F32),
        vm((width, n), BF16), vm((width, n), BF16), vm((n, width), BF16), vm((n, width), BF16),
        vm((4 * CORNER, k), BF16), vm((4 * CORNER, k), BF16),
        vm((k, 4 * CORNER), BF16), vm((k, 4 * CORNER), BF16),
        vm((cols * k, rows * k), BF16), vm((cols * k, rows * k), BF16),
        vm((n, r), F32),
        vm((4, k, share), F32), vm((4, k, share), F32),
        vm((2 * STEPS + 1, slot_count, r), F32), vm((2 * STEPS + 1, slot_pad, r), F32),
        vm((2 * STEPS, width - k, r), F32), vm((2 * STEPS, width - k, r), F32),
        vm((STEPS, rows, k, r), F32),
        vm((STEPS, cols, k, r), F32), vm((STEPS, cols, k, r), F32),
        dma((2,)), dma((4,)), dma((4,)),
        dma((2 * STEPS + 1, 8)), dma((2 * STEPS + 1, 8)),
        dma((2 * STEPS, 8)), dma((2 * STEPS, 8)),
        dma((STEPS, rows)), dma((STEPS, rows)),
        dma((STEPS, cols)), dma((STEPS, cols)),
    ]
    in_vmem = pl.BlockSpec(memory_space=pltpu.VMEM)
    in_place = pl.BlockSpec(memory_space=pl.ANY)
    iterate, residual = pl.pallas_call(
        functools.partial(kernel, rows, cols, n, r, k, share),
        out_shape=[jax.ShapeDtypeStruct((n, r), F32)] * 2,
        in_specs=[in_vmem, in_place, in_place, in_vmem, in_vmem, in_vmem, in_vmem],
        out_specs=[in_vmem] * 2,
        scratch_shapes=scratch,
        compiler_params=pltpu.CompilerParams(
            collective_id=0, has_side_effects=True, vmem_limit_bytes=60 * 2**20
        ),
    )(
        local_load[0, 0],
        schur_operator[0, 0],
        local_solver[0, 0],
        coarse_modes[0, 0],
        coarse_inverse[0, 0].reshape(rows * k, cols * k),
        slots[None, :],
        weight[None, :],
    )
    return (iterate[None, None], residual[None, None])


def solution(mesh):
    rows, cols = mesh.shape["row"], mesh.shape["col"]
    in_specs = (
        P("row", "col", None, None),
        P("row", "col", None, None),
        P("row", "col", None, None),
        P("row", "col", None, None),
        P("row", "col", None, None, None),
        P("row", "col", None, None, None),
        P("row", "col", None, None),
        P("row", "col", None),
    )
    out_specs = (P("row", "col", None, None), P("row", "col", None, None))
    return jax.shard_map(
        functools.partial(on_device, rows, cols),
        mesh=mesh, in_specs=in_specs, out_specs=out_specs, check_vma=False,
    )
```

```python
import functools

import jax
import jax.numpy as jnp
from jax import lax
from jax.experimental import pallas as pl
from jax.experimental.pallas import tpu as pltpu
from jax.sharding import PartitionSpec as P

CORNER = 16
STEPS = 2
F32 = jnp.float32
BF16 = jnp.bfloat16
MESH = pl.DeviceIdType.MESH

DIRS = ((0, -1), (0, 1), (-1, 0), (1, 0), (-1, -1), (-1, 1), (1, -1), (1, 1))
OPPOSITE = (1, 0, 3, 2, 7, 6, 5, 4)
SIDES = (0, 1)
OTHERS = (4, 5, 6, 7, 2, 3)
LANES = 128


def split(value):
    high = value.astype(BF16)
    low = (value - high.astype(F32)).astype(BF16)
    return high, low


def dot(left, right):
    return jnp.dot(left, right, preferred_element_type=F32)


def dot3(left, right):
    (lh, ll), (rh, rl) = left, right
    return dot(lh, rh) + (dot(lh, rl) + dot(ll, rh))


def put(refs, value):
    refs[0][...], refs[1][...] = split(value)


def get(refs, *where):
    return tuple(ref[where] if where else ref[...] for ref in refs)


def pick(onehot, value):
    high, low = value
    return dot(onehot, high) + dot(onehot, low)


def kernel(
    rows, cols, n, r, k, share,
    load_hbm, schur_hbm, solver_hbm, modes_ref, tile_ref, slots_ref, mult_ref,
    iter_ref, res_ref,
    mat_s, mat_m, load_ref, gather_ref, scatter_ref, wide_ref,
    s2, m2, ext, ext_t, cor, cor_t, tile_t, se, st, mt, gse, gst, gmt, es, est,
    local_ref, packet_ref, rest_ref, solved_ref, own_ref, moved_ref,
    mode_send, mode_recv, a_send, a_recv, x_send, x_recv, gat, part, red,
    local_sem, mode_ss, mode_rs, a_ss, a_rs, x_ss, x_rs, g_ss, g_rs, p_ss, p_rs,
):
    a = lax.axis_index("row")
    b = lax.axis_index("col")
    copy_l = pltpu.make_async_copy(load_hbm, load_ref, local_sem.at[0])
    copy_s = pltpu.make_async_copy(schur_hbm, mat_s, local_sem.at[1])
    copy_m = pltpu.make_async_copy(solver_hbm, mat_m, local_sem.at[2])
    copy_l.start()
    copy_s.start()
    copy_m.start()

    def exists(d):
        p, q = a + DIRS[d][0], b + DIRS[d][1]
        return (p >= 0) & (p < rows) & (q >= 0) & (q < cols)

    def there(d):
        return (a + DIRS[d][0], b + DIRS[d][1])

    mode_recv[...] = jnp.zeros_like(mode_recv)
    a_recv[...] = jnp.zeros_like(a_recv)
    x_recv[...] = jnp.zeros_like(x_recv)

    barrier = pltpu.get_barrier_semaphore()
    for off in range(1, rows):
        pl.semaphore_signal(
            barrier, inc=1, device_id=(lax.rem(a + off, rows), b), device_id_type=MESH
        )
    for off in range(1, cols):
        pl.semaphore_signal(
            barrier, inc=1, device_id=(a, lax.rem(b + off, cols)), device_id_type=MESH
        )
    for d in range(4, 8):
        @pl.when(exists(d))
        def _():
            pl.semaphore_signal(barrier, inc=1, device_id=there(d), device_id_type=MESH)

    slot_pad = slots_ref.shape[1]
    slots = slots_ref[...]
    scatter_ref[...] = jnp.where(
        lax.broadcasted_iota(jnp.int32, (n, slot_pad), 0).astype(F32) == slots, 1.0, 0.0
    ).astype(BF16)
    weight = 1.0 / mult_ref[...].astype(F32)
    zw = modes_ref[...] * weight
    zw2 = split(zw)
    sides = scatter_ref[:, 0:4 * share]
    at_slots = dot(zw2[0], sides) + dot(zw2[1], sides)
    for d in range(4):
        mode_send[d] = at_slots[:, d * share:(d + 1) * share]

    diagonals = sum(exists(d).astype(jnp.int32) for d in range(4, 8))
    pl.semaphore_wait(barrier, rows + cols - 2 + diagonals)
    pending = []

    def for_dirs(dirs, body):
        for d in dirs:
            @pl.when(exists(d))
            def _():
                body(d)

    def mode_copy(d, out):
        e = OPPOSITE[d] if out else d
        return pltpu.make_async_remote_copy(
            src_ref=mode_send.at[d],
            dst_ref=mode_recv.at[e],
            send_sem=mode_ss.at[d],
            recv_sem=mode_rs.at[e],
            device_id=there(d),
            device_id_type=MESH,
        )

    for_dirs(range(4), lambda d: mode_copy(d, True).start())
    pending.append(lambda: for_dirs(range(4), lambda d: mode_copy(d, True).wait_send()))

    def exchange(send, recv, ss, rs, wide):
        def span(d):
            if d < 4:
                return pl.ds(d * wide, wide)
            return pl.ds(4 * wide + (d - 4) * CORNER, CORNER)

        def copy(d, out):
            e = OPPOSITE[d] if out else d
            return pltpu.make_async_remote_copy(
                src_ref=send.at[span(d)],
                dst_ref=recv.at[span(e)],
                send_sem=ss.at[d],
                recv_sem=rs.at[e],
                device_id=there(d),
                device_id_type=MESH,
            )

        pending.append(lambda: for_dirs(range(8), lambda d: copy(d, True).wait_send()))

        def start(dirs):
            for_dirs(dirs, lambda d: copy(d, True).start())

        def wait(dirs):
            for_dirs(dirs, lambda d: copy(d, False).wait_recv())

        return start, wait

    slot_count = 4 * share + 4 * CORNER
    near = (slice(None), slice(0, 2 * share))
    far = (slice(None), slice(2 * share, slot_pad))

    slots_t = jnp.broadcast_to(slots, (LANES, slot_pad)).T
    for i in range(n // LANES):
        ids = (lax.broadcasted_iota(jnp.int32, (slot_pad, LANES), 1) + i * LANES).astype(F32)
        gather_ref[:, i * LANES:(i + 1) * LANES] = jnp.where(ids == slots_t, 1.0, 0.0).astype(BF16)
    corner_g = gather_ref[4 * share:slot_count, :]
    corner_m = pick(corner_g, split(zw.T))
    put(cor, corner_m)
    put(cor_t, corner_m.T)
    copy_l.wait()
    local_ref[...] = -load_ref[...]
    ext[0][0:k, :] = zw2[0]
    ext[1][0:k, :] = zw2[1]
    ext[0][5 * k:, :] = corner_g
    ext[1][5 * k:, :] = jnp.zeros_like(corner_g)
    for_dirs(range(4), lambda d: mode_copy(d, False).wait_recv())
    for d in range(4):
        m_h, m_l = split(mode_recv[d])
        onehot = gather_ref[d * share:(d + 1) * share, :]
        ext[0][(d + 1) * k:(d + 2) * k, :] = dot(m_h, onehot).astype(BF16)
        ext[1][(d + 1) * k:(d + 2) * k, :] = dot(m_l, onehot).astype(BF16)

    def prepare_a():
        weight_t = jnp.broadcast_to(weight, (LANES, n)).T
        for i in range(r // LANES):
            wide_ref[:, i * LANES:(i + 1) * LANES] = weight_t
        put(tile_t, tile_ref[...].T)
        for i in range(2):
            ext_t[i][...] = ext[i][...].astype(F32).T.astype(BF16)
        packet_ref[...] = pick(gather_ref[0:slot_count, :], split(local_ref[...]))
        copy_s.wait()
        put(s2, mat_s[...])

    def prepare_b():
        put(se, dot3(get(s2), get(ext_t)))
        copy_m.wait()
        put(m2, mat_m[...])

    def prepare_c():
        for i in range(2):
            gse[i][...] = dot(gather_ref[0:slot_count, :], se[i][...]).astype(BF16)
            mt[i][...] = dot(m2[i][...], scatter_ref[...]).astype(BF16)
            gmt[i][...] = dot(gather_ref[0:slot_count, :], mt[i][...]).astype(BF16)

    def prepare_d():
        for i in range(2):
            st[i][...] = dot(s2[i][...], scatter_ref[...]).astype(BF16)
            gst[i][...] = dot(gather_ref[0:slot_count, :], st[i][...]).astype(BF16)

    def prepare_e():
        put(es, dot3(get(ext), get(s2)))
        for i in range(2):
            est[i][...] = dot(es[i][...], scatter_ref[...]).astype(BF16)

    def send_slots(index, base, left, right):
        send, recv = a_send.at[index], a_recv.at[index]
        start, wait = exchange(send, recv, a_ss.at[index], a_rs.at[index], share)
        first, second = pl.ds(0, 2 * share), pl.ds(2 * share, slot_count - 2 * share)
        send[first, :] = base[first, :] + dot3(get(left, first), right)
        start(SIDES)
        send[second, :] = base[second, :] + dot3(get(left, second), right)
        start(OTHERS)
        return recv, wait

    out = dot3(get(ext), split(local_ref[...]))
    for t in range(STEPS):
        gat_t, part_t, red_t = gat.at[t], part.at[t], red.at[t]
        send, recv = x_send.at[2 * t], x_recv.at[2 * t]
        start, wait = exchange(send, recv, x_ss.at[2 * t], x_rs.at[2 * t], k)
        send[...] = out[k:, :]
        start((4, 5, 6, 7, 0, 1, 2, 3))
        own = -out[0:k, :]
        if t == 0:
            prepare_a()
        else:
            own = own + dot3(get(ext, slice(0, k)), split(res_ref[...]))
            iter_ref[...] += own_ref[...] + pick(scatter_ref[...], arrived)
            local_ref[...] = moved_ref[...] + dot3(get(st), arrived)
            packet_ref[...] = pick(gather_ref[0:slot_count, :], split(local_ref[...]))
        wait(range(8))
        total = recv[0:k, :]
        for d in range(1, 4):
            total = total + recv[d * k:(d + 1) * k, :]
        total = total + dot3(get(cor_t), split(recv[4 * k:, :]))
        gat_t[a] = own - total

        def gather_copy(off, out, t=t, gat_t=gat_t):
            peer = lax.rem(a + off, rows) if out else lax.rem(a + rows - off, rows)
            return pltpu.make_async_remote_copy(
                src_ref=gat_t.at[a],
                dst_ref=gat_t.at[a if out else peer],
                send_sem=g_ss.at[t, off],
                recv_sem=g_rs.at[t, off],
                device_id=(peer, b),
                device_id_type=MESH,
            )

        for off in range(1, rows):
            gather_copy(off, True).start()
            pending.append(lambda off=off, gather_copy=gather_copy: gather_copy(off, True).wait_send())
        if t == 0:
            prepare_b()
        for off in range(1, rows):
            gather_copy(off, False).wait_recv()
        rhs = split(gat_t[...].reshape(rows * k, r))
        part_t[...] = dot3(get(tile_t), rhs).reshape(cols, k, r)

        def part_copy(off, out, t=t, part_t=part_t, red_t=red_t):
            peer = lax.rem(b + off, cols) if out else lax.rem(b + cols - off, cols)
            return pltpu.make_async_remote_copy(
                src_ref=part_t.at[peer],
                dst_ref=red_t.at[off],
                send_sem=p_ss.at[t, off],
                recv_sem=p_rs.at[t, off],
                device_id=(a, peer),
                device_id_type=MESH,
            )

        for off in range(1, cols):
            part_copy(off, True).start()
            pending.append(lambda off=off, part_copy=part_copy: part_copy(off, True).wait_send())
        if t == 0:
            prepare_c()
        sol = part_t[b]
        for off in range(1, cols):
            part_copy(off, False).wait_recv()
            sol = sol + red_t[off]

        send, recv = x_send.at[2 * t + 1], x_recv.at[2 * t + 1]
        start, wait = exchange(send, recv, x_ss.at[2 * t + 1], x_rs.at[2 * t + 1], k)
        send[4 * k:, :] = dot3(get(cor), split(sol))
        start((4, 5, 6, 7))
        for d in range(4):
            send[d * k:(d + 1) * k, :] = sol
        start((0, 1, 2, 3))
        if t == 0:
            prepare_d()
        wait(range(8))
        all_sol = split(jnp.concatenate([sol, recv[...]], axis=0))

        recv, wait = send_slots(2 * t, packet_ref, gse, all_sol)
        rest = -(local_ref[...] + dot3(get(se), all_sol))
        if t > 0:
            rest = rest + res_ref[...]
        rest_ref[...] = rest
        solved = dot3(get(m2), split(wide_ref[...] * rest))
        solved_ref[...] = solved
        packet_ref[...] = 0.5 * pick(gather_ref[0:slot_count, :], split(solved))
        corr = dot3(get(ext_t), all_sol)
        iter_ref[...] = corr if t == 0 else iter_ref[...] + corr
        if t == 0:
            prepare_e()
        wait(OTHERS)
        more = split(recv[2 * share:, :])
        packet_ref[...] -= 0.25 * dot3(get(gmt, *far), more)
        wait(SIDES)
        less = split(-0.25 * recv[0:2 * share, :])
        back = recv
        recv, wait = send_slots(2 * t + 1, packet_ref, tuple(ref.at[near] for ref in gmt), less)

        old = split(back[...])
        res_ref[...] = rest_ref[...] - pick(scatter_ref[...], old)
        own_solved = wide_ref[...] * (solved_ref[...] - 0.5 * dot3(get(mt), old))
        own_ref[...] = own_solved
        own_2 = split(own_solved)
        moved_ref[...] = dot3(get(s2), own_2)
        if t < STEPS - 1:
            out = dot3(get(es), own_2)
        else:
            packet_ref[...] = pick(gather_ref[0:slot_count, :], split(moved_ref[...]))
        wait(OTHERS)
        more = split(recv[2 * share:, :])
        if t < STEPS - 1:
            out = out + dot3(get(est, *far), more)
            wait(SIDES)
            out = out + dot3(get(est, *near), split(recv[0:2 * share, :]))
            arrived = split(recv[...])
        else:
            packet_ref[...] += dot3(get(gst, *far), more)
            wait(SIDES)
            less = split(recv[0:2 * share, :])
            last, wait_last = send_slots(
                2 * STEPS, packet_ref, tuple(ref.at[near] for ref in gst), less
            )
            arrived = split(recv[...])
            iter_ref[...] += own_ref[...] + pick(scatter_ref[...], arrived)
            res_ref[...] -= moved_ref[...] + dot3(get(st), arrived)
            wait_last(range(8))
            res_ref[...] -= pick(scatter_ref[...], split(last[...]))
    for wait_sent in pending:
        wait_sent()


def on_device(
    rows, cols,
    local_load,
    schur_operator,
    local_solver,
    coarse_modes,
    coarse_inverse,
    share_rows,
    share_count,
    multiplicity,
):
    n, r = local_load.shape[2:]
    k = coarse_modes.shape[2]
    share = share_rows.shape[-1]
    live = lax.broadcasted_iota(jnp.int32, share_rows.shape[2:], 2) < share_count[0, 0][..., None]
    listed = jnp.where(live, share_rows[0, 0], -1).astype(F32)
    pieces = [
        listed[p + 1, q + 1, : share if d < 4 else CORNER] for d, (p, q) in enumerate(DIRS)
    ]
    slot_count = 4 * share + 4 * CORNER
    slot_pad = -(-slot_count // LANES) * LANES
    slots = jnp.pad(jnp.concatenate(pieces), (0, slot_pad - slot_count), constant_values=-1.0)
    width = 5 * k + 4 * CORNER
    vm = pltpu.VMEM
    dma = pltpu.SemaphoreType.DMA
    def pair(*shape):
        return [vm(shape, BF16), vm(shape, BF16)]

    scratch = [
        vm((n, n), F32), vm((n, n), F32), vm((n, r), F32),
        vm((slot_pad, n), BF16), vm((n, slot_pad), BF16), vm((n, r), F32),
        pair(n, n), pair(n, n), pair(width, n), pair(n, width),
        pair(4 * CORNER, k), pair(k, 4 * CORNER), pair(cols * k, rows * k),
        pair(n, width), pair(n, slot_pad), pair(n, slot_pad),
        pair(slot_count, width), pair(slot_count, slot_pad), pair(slot_count, slot_pad),
        pair(width, n), pair(width, slot_pad),
        vm((n, r), F32), vm((slot_count, r), F32), vm((n, r), F32), vm((n, r), F32),
        vm((n, r), F32), vm((n, r), F32),
        vm((4, k, share), F32), vm((4, k, share), F32),
        vm((2 * STEPS + 1, slot_count, r), F32), vm((2 * STEPS + 1, slot_pad, r), F32),
        vm((2 * STEPS, width - k, r), F32), vm((2 * STEPS, width - k, r), F32),
        vm((STEPS, rows, k, r), F32),
        vm((STEPS, cols, k, r), F32), vm((STEPS, cols, k, r), F32),
        dma((3,)), dma((4,)), dma((4,)),
        dma((2 * STEPS + 1, 8)), dma((2 * STEPS + 1, 8)),
        dma((2 * STEPS, 8)), dma((2 * STEPS, 8)),
        dma((STEPS, rows)), dma((STEPS, rows)),
        dma((STEPS, cols)), dma((STEPS, cols)),
    ]
    in_vmem = pl.BlockSpec(memory_space=pltpu.VMEM)
    in_place = pl.BlockSpec(memory_space=pl.ANY)
    iterate, residual = pl.pallas_call(
        functools.partial(kernel, rows, cols, n, r, k, share),
        out_shape=[jax.ShapeDtypeStruct((n, r), F32)] * 2,
        in_specs=[in_place, in_place, in_place, in_vmem, in_vmem, in_vmem, in_vmem],
        out_specs=[in_vmem] * 2,
        scratch_shapes=scratch,
        compiler_params=pltpu.CompilerParams(
            collective_id=0, has_side_effects=True, vmem_limit_bytes=60 * 2**20
        ),
    )(
        local_load[0, 0],
        schur_operator[0, 0],
        local_solver[0, 0],
        coarse_modes[0, 0],
        coarse_inverse[0, 0].reshape(rows * k, cols * k),
        slots[None, :],
        multiplicity[0],
    )
    return (iterate[None, None], residual[None, None])


def solution(mesh):
    rows, cols = mesh.shape["row"], mesh.shape["col"]
    in_specs = (
        P("row", "col", None, None),
        P("row", "col", None, None),
        P("row", "col", None, None),
        P("row", "col", None, None),
        P("row", "col", None, None, None),
        P("row", "col", None, None, None),
        P("row", "col", None, None),
        P("row", "col", None),
    )
    out_specs = (P("row", "col", None, None), P("row", "col", None, None))
    return jax.shard_map(
        functools.partial(on_device, rows, cols),
        mesh=mesh, in_specs=in_specs, out_specs=out_specs, check_vma=False,
    )
```
